128 devices in a mesh: grp: 4 (over y), dev: 32 (over z, x, core).
Axes of the slice: x: 4, y: 4, z: 4, core: 2. Of those that a mesh axis runs over, the one named last changes fastest.
Arguments:
- embeddings: bfloat16 [32768, 768], P(('grp', 'dev'))
- cluster_id: int32 [32768], P(('grp', 'dev')), may hold values from 0 to 31, as said below
Outputs:
- max_similarity: float32 [32768], P(('grp', 'dev'))
The draws below stay inside these ranges and needn't reach their ends.
Inputs may be any that keep to these rules, and one draw needn't show every extreme that they name: `cluster_id`: cluster c is owned by group c mod the number of groups. In each aligned block of 256 rows (the rows of one device), at most 128 rows have clusters owned by one group, and exactly 128 rows for some group in every block.
All inputs are finite; a program needn't handle non-finite values.
Results may differ from the reference program's by a relative error of at most 0.0065.
Values may be sent and summed in bfloat16 or wider, within the bound.
No kernel may reach another device: no remote copies, remote signals or barrier semaphores. Data moves between devices by JAX's collectives and lax.ppermute only.
A program may use at most 64 MiB of HBM per device.

```python
import jax
import jax.numpy as jnp
from jax import lax

D = 768
CLUSTERS = 32
ROWS_DEV = 256
SLOT = 128
TOKENS = 32768
N_GRP = 4


def cluster_layout(key):
    cpg = CLUSTERS // N_GRP
    blocks = TOKENS // ROWS_DEV
    order_local = jax.random.permutation(jax.random.fold_in(key, 101), cpg).astype(jnp.int32)
    first = jax.random.randint(jax.random.fold_in(key, 102), (blocks, 1), 0, N_GRP)
    other = jax.random.randint(jax.random.fold_in(key, 103), (blocks, ROWS_DEV), 1, N_GRP)
    position = jnp.arange(ROWS_DEV, dtype=jnp.int32)[None, :]
    owner = jnp.where(position < SLOT, first, (first + other) % N_GRP).astype(jnp.int32)
    shuffle_keys = jax.random.split(jax.random.fold_in(key, 104), blocks)
    owner = jax.vmap(lambda k, row: jax.random.permutation(k, row))(shuffle_keys, owner)
    local_a = jax.random.randint(jax.random.fold_in(key, 105), (blocks, ROWS_DEV), 0, cpg)
    local_b = jax.random.randint(jax.random.fold_in(key, 106), (blocks, ROWS_DEV), 0, cpg)
    local = order_local[jnp.minimum(local_a, local_b)]
    ids = (local * N_GRP + owner).reshape(TOKENS).astype(jnp.int32)
    return ids


def draw_cluster_id(key, part):
    return cluster_layout(key)


def draw_embeddings(key, part):
    ids = cluster_layout(key)
    key = jax.random.fold_in(key, 7)
    centers = jax.random.normal(jax.random.fold_in(key, 1), (CLUSTERS, D), jnp.float32)
    noise = jax.random.normal(jax.random.fold_in(key, 2), (TOKENS, D), jnp.float32)
    values = 0.9 * centers[ids] + noise
    return values.astype(jnp.bfloat16)


def setup_inputs(seed: int = 0) -> dict:
    key_list = jax.random.split(jax.random.key(seed), 3)
    return {
        "embeddings": draw_embeddings(jax.random.fold_in(key_list[2], 71), 0),
        "cluster_id": draw_cluster_id(jax.random.fold_in(key_list[2], 71), 0),
    }


def reference(embeddings, cluster_id):
    values = embeddings.astype(jnp.float32)
    normed = (values / jnp.sqrt(lax.optimization_barrier(jnp.sum(values * values, axis=1, keepdims=True)) + 1e-06)).astype(jnp.bfloat16)
    width = ROWS_DEV * 8
    blocks = TOKENS // width
    all_index = jnp.arange(TOKENS, dtype=jnp.int32)

    def one_block(index):
        begin = (index * width).astype(jnp.int32)
        rows = lax.dynamic_slice_in_dim(normed, begin, width, 0)
        row_ids = lax.dynamic_slice_in_dim(cluster_id, begin, width, 0)
        row_index = begin + jnp.arange(width, dtype=jnp.int32)
        scores = jnp.dot(rows, normed.T, preferred_element_type=jnp.float32)
        match = (row_ids[:, None] == cluster_id[None, :]) & (row_index[:, None] != all_index[None, :])
        return lax.optimization_barrier(jnp.max(jnp.where(match, scores, jnp.float32(-1.0)), axis=1))
    result = lax.map(one_block, jnp.arange(blocks, dtype=jnp.int32))
    return result.reshape(TOKENS)
```

```python
import functools

import jax
import jax.numpy as jnp
from jax import lax
from jax.experimental import pallas as pl
from jax.experimental.pallas import tpu as pltpu
from jax.sharding import PartitionSpec as P

AXES = ("grp", "dev")
ROWS = 256
TAIL = 16
HALF = ROWS + TAIL
BLOCK = HALF + ROWS
SECOND = HALF
LANES = 128
FLOOR = -1.0


def pack_kernel(own_ref, other_ref, own_ids_ref, other_ids_ref, block_ref, half_ref):
    def unit(ref):
        values = ref[...].astype(jnp.float32)
        norm = jnp.sqrt(jnp.sum(values * values, axis=1, keepdims=True) + 1e-06)
        return (values / norm).astype(jnp.bfloat16)

    own = unit(own_ref)
    own_ids = jnp.broadcast_to(own_ids_ref[...].astype(jnp.float32), (TAIL, ROWS)).astype(jnp.bfloat16)
    other_ids = jnp.broadcast_to(other_ids_ref[...].astype(jnp.float32), (TAIL, ROWS)).astype(jnp.bfloat16)
    rest = jnp.zeros((TAIL, own.shape[1] - 2 * ROWS), jnp.bfloat16)
    for ref in (block_ref, half_ref):
        ref[0:ROWS, :] = own
        ref[ROWS:HALF, 0:ROWS] = own_ids
        ref[ROWS:HALF, ROWS : 2 * ROWS] = other_ids
        ref[ROWS:HALF, 2 * ROWS :] = rest
    block_ref[SECOND:BLOCK, :] = unit(other_ref)


def pack(own, other, own_ids, other_ids):
    width = own.shape[1]
    return pl.pallas_call(
        pack_kernel,
        out_shape=(
            jax.ShapeDtypeStruct((BLOCK, width), jnp.bfloat16),
            jax.ShapeDtypeStruct((HALF, width), jnp.bfloat16),
        ),
        compiler_params=pltpu.CompilerParams(vmem_limit_bytes=16 * 1024 * 1024),
        name="pack",
    )(own, other, own_ids.reshape(1, ROWS), other_ids.reshape(1, ROWS))


def parts_of(ref):
    return [(0, 0)] if ref.shape[0] == HALF else [(0, 0), (SECOND, ROWS)]


def ids_row(ref, lane):
    return ref[ROWS:HALF, lane : lane + ROWS].astype(jnp.float32)[0:1, :]


def score_kernel(n_queries, n_keys, first, last, *refs):
    queries, refs = refs[:n_queries], refs[n_queries:]
    keys, refs = refs[:n_keys], refs[n_keys:]
    query_parts = [(ref, row, lane) for ref in queries for row, lane in parts_of(ref)]
    if first:
        best_ref, column_ref = refs
        row_index = lax.broadcasted_iota(jnp.int32, (ROWS, ROWS), 0)
        col_index = lax.broadcasted_iota(jnp.int32, (ROWS, ROWS), 1)
        for place, (ref, row, lane) in enumerate(query_parts):
            ids = jnp.broadcast_to(ids_row(ref, lane), (ROWS, ROWS))
            column = jnp.sum(jnp.where(row_index == col_index, ids, 0.0), axis=1, keepdims=True)
            column_ref[place * ROWS : (place + 1) * ROWS, :] = jnp.broadcast_to(column, (ROWS, LANES))
    elif last:
        before_ref, column_ref, out_ref, best_ref = refs
    else:
        before_ref, column_ref, best_ref = refs

    for place, (ref, row, lane) in enumerate(query_parts):
        here = slice(place * ROWS, (place + 1) * ROWS)
        rows = ref[row : row + ROWS, :]
        column = column_ref[here, :]
        best = jnp.full((ROWS, LANES), FLOOR, jnp.float32) if first else before_ref[here, :]
        for number, key_ref in enumerate(keys):
            for key_row, key_lane in parts_of(key_ref):
                scores = lax.dot_general(
                    rows,
                    key_ref[key_row : key_row + ROWS, :],
                    (((1,), (1,)), ((), ())),
                    preferred_element_type=jnp.float32,
                )
                ids = ids_row(key_ref, key_lane)
                for start in range(0, ROWS, LANES):
                    match = column == ids[:, start : start + LANES]
                    if first and place == 0 and number == 0 and key_row == 0:
                        match = match & (
                            row_index[:, start : start + LANES] != col_index[:, start : start + LANES]
                        )
                    best = jnp.maximum(best, jnp.where(match, scores[:, start : start + LANES], FLOOR))
        if last:
            out_ref[0:1, here] = jnp.max(best.T, axis=0, keepdims=True)
        else:
            best_ref[here, :] = best


def score(queries, keys, state=None, last=False):
    count = sum(len(parts_of(q)) for q in queries) * ROWS
    wide = jax.ShapeDtypeStruct((count, LANES), jnp.float32)
    first = state is None
    shapes = (wide, wide) if first else wide
    scratch = []
    if last:
        shapes = jax.ShapeDtypeStruct((1, count), jnp.float32)
        scratch = [pltpu.VMEM((8, LANES), jnp.float32)]
    key_rows = sum(len(parts_of(k)) for k in keys) * ROWS
    width = keys[0].shape[1]
    result = pl.pallas_call(
        functools.partial(score_kernel, len(queries), len(keys), first, last),
        out_shape=shapes,
        scratch_shapes=scratch,
        compiler_params=pltpu.CompilerParams(vmem_limit_bytes=32 * 1024 * 1024),
        cost_estimate=pl.CostEstimate(
            flops=2 * count * key_rows * width,
            bytes_accessed=2 * width * (count + key_rows),
            transcendentals=0,
        ),
        name="score",
    )(*queries, *keys, *(() if first else state))
    if last:
        return result
    return result if first else (result, state[1])


def per_device(embeddings, cluster_id):
    ny, nz, nx = 4, 4, 4

    def place(y, z, x, core):
        return (((y % ny) * nz + z % nz) * nx + x % nx) * 2 + core

    def fetch(value, *offsets):
        pairs = []
        for y in range(ny):
            for z in range(nz):
                for x in range(nx):
                    for core, (dy, dz, dx) in enumerate(offsets):
                        pairs.append((place(y + dy, z + dz, x + dx, core), place(y, z, x, core)))
        return lax.ppermute(value, AXES, pairs)

    def give(value, *offsets):
        return fetch(value, *(tuple(-o for o in offset) for offset in offsets))

    def swap(value):
        return lax.ppermute(value, AXES, [(i, i ^ 1) for i in range(ny * nz * nx * 2)])

    block, half = pack(embeddings, swap(embeddings), cluster_id, swap(cluster_id))

    key1 = fetch(block, (0, 0, 1), (0, 1, 0))
    key2 = fetch(block, (0, 0, -1), (0, -1, 0))
    near = fetch(block, (1, 0, 0), (-1, 0, 0))
    key3 = fetch(block, (0, 0, 2), (0, 2, 0))
    far = fetch(half, (2, 0, 0), (2, 0, 0))
    key4 = fetch(key1, (0, 1, 0), (0, 0, -1))
    key5 = fetch(key2, (0, -1, 0), (0, 0, 1))
    key6 = fetch(key3, (0, 1, 0), (0, 0, 1))
    key7 = fetch(key3, (0, -1, 0), (0, 0, -1))
    key8 = fetch(key3[:HALF], (0, 2, 0), (0, 0, 2))

    queries = [half, far, near]
    state = score(queries, [block, key1, key2, swap(key1), swap(key2)])
    state = score(queries, [key3, swap(key3), key4, swap(key4), key5, swap(key5)], state)
    state = score(queries, [key6, swap(key6)], state)
    best = score(queries, [key7, swap(key7), key8, swap(key8)], state, last=True)[0]

    from_near = give(best[2 * ROWS :], (1, 0, 0), (-1, 0, 0))
    from_far = give(best[ROWS : 2 * ROWS], (2, 0, 0), (2, 0, 0))
    mine = jnp.maximum(best[:ROWS], jnp.maximum(from_far, from_near[:ROWS]))
    return jnp.maximum(mine, swap(from_near[ROWS:]))


def solution(mesh):
    in_specs = (P(AXES, None), P(AXES))
    return jax.shard_map(
        per_device, mesh=mesh, in_specs=in_specs, out_specs=P(AXES), check_vma=False
    )
```

```python
import functools

import jax
import jax.numpy as jnp
from jax import lax
from jax.experimental import pallas as pl
from jax.experimental.pallas import tpu as pltpu
from jax.sharding import PartitionSpec as P

AXES = ("grp", "dev")
ROWS = 256
TAIL = 16
HALF = ROWS + TAIL
BLOCK = HALF + ROWS
SECOND = HALF
LANES = 128
FLOOR = -1.0


def pack_kernel(own_ref, other_ref, own_ids_ref, other_ids_ref, block_ref, half_ref):
    def unit(ref):
        values = ref[...].astype(jnp.float32)
        norm = jnp.sqrt(jnp.sum(values * values, axis=1, keepdims=True) + 1e-06)
        return (values / norm).astype(jnp.bfloat16)

    own = unit(own_ref)
    own_ids = jnp.broadcast_to(own_ids_ref[...].astype(jnp.float32), (TAIL, ROWS)).astype(jnp.bfloat16)
    other_ids = jnp.broadcast_to(other_ids_ref[...].astype(jnp.float32), (TAIL, ROWS)).astype(jnp.bfloat16)
    rest = jnp.zeros((TAIL, own.shape[1] - 2 * ROWS), jnp.bfloat16)
    for ref in (block_ref, half_ref):
        ref[0:ROWS, :] = own
        ref[ROWS:HALF, 0:ROWS] = own_ids
        ref[ROWS:HALF, ROWS : 2 * ROWS] = other_ids
        ref[ROWS:HALF, 2 * ROWS :] = rest
    block_ref[SECOND:BLOCK, :] = unit(other_ref)


def pack(own, other, own_ids, other_ids):
    width = own.shape[1]
    return pl.pallas_call(
        pack_kernel,
        out_shape=(
            jax.ShapeDtypeStruct((BLOCK, width), jnp.bfloat16),
            jax.ShapeDtypeStruct((HALF, width), jnp.bfloat16),
        ),
        compiler_params=pltpu.CompilerParams(vmem_limit_bytes=16 * 1024 * 1024),
        name="pack",
    )(own, other, own_ids.reshape(1, ROWS), other_ids.reshape(1, ROWS))


OWN, OTHER = (0, 0), (SECOND, ROWS)


def whole(block):
    return (block, (OWN,) if block.shape[0] == HALF else (OWN, OTHER))


def ids_row(ref, lane):
    return ref[ROWS:HALF, lane : lane + ROWS].astype(jnp.float32)[0:1, :]


def score_kernel(query_parts, key_parts, n_blocks, first, last, *refs):
    blocks, refs = refs[:n_blocks], refs[n_blocks:]
    query_parts = [(blocks[at], row, lane) for at, (row, lane) in query_parts]
    key_parts = [(blocks[at], row, lane) for at, (row, lane) in key_parts]
    if first:
        best_ref, column_ref = refs
        row_index = lax.broadcasted_iota(jnp.int32, (ROWS, ROWS), 0)
        col_index = lax.broadcasted_iota(jnp.int32, (ROWS, ROWS), 1)
        for place, (ref, row, lane) in enumerate(query_parts):
            ids = jnp.broadcast_to(ids_row(ref, lane), (ROWS, ROWS))
            column = jnp.sum(jnp.where(row_index == col_index, ids, 0.0), axis=1, keepdims=True)
            column_ref[place * ROWS : (place + 1) * ROWS, :] = jnp.broadcast_to(column, (ROWS, LANES))
    elif last:
        before_ref, column_ref, out_ref = refs
    else:
        before_ref, column_ref, best_ref = refs

    for place, (ref, row, lane) in enumerate(query_parts):
        here = slice(place * ROWS, (place + 1) * ROWS)
        rows = ref[row : row + ROWS, :]
        column = column_ref[here, :]
        best = jnp.full((ROWS, LANES), FLOOR, jnp.float32) if first else before_ref[here, :]
        for number, (key_ref, key_row, key_lane) in enumerate(key_parts):
            scores = lax.dot_general(
                rows,
                key_ref[key_row : key_row + ROWS, :],
                (((1,), (1,)), ((), ())),
                preferred_element_type=jnp.float32,
            )
            ids = ids_row(key_ref, key_lane)
            for start in range(0, ROWS, LANES):
                match = column == ids[:, start : start + LANES]
                if first and place == 0 and number == 0:
                    match = match & (
                        row_index[:, start : start + LANES] != col_index[:, start : start + LANES]
                    )
                best = jnp.maximum(best, jnp.where(match, scores[:, start : start + LANES], FLOOR))
        if last:
            out_ref[0:1, here] = jnp.max(best.T, axis=0, keepdims=True)
        else:
            best_ref[here, :] = best


def score(queries, keys, state=None, last=False):
    blocks = []

    def listed(pieces):
        found = []
        for block, parts in pieces:
            at = next((i for i, b in enumerate(blocks) if b is block), len(blocks))
            if at == len(blocks):
                blocks.append(block)
            found += [(at, part) for part in parts]
        return found

    query_parts, key_parts = listed(queries), listed(keys)
    count, key_rows, width = len(query_parts) * ROWS, len(key_parts) * ROWS, blocks[0].shape[1]
    wide = jax.ShapeDtypeStruct((count, LANES), jnp.float32)
    first = state is None
    shapes = (wide, wide) if first else wide
    if last:
        shapes = jax.ShapeDtypeStruct((1, count), jnp.float32)
    result = pl.pallas_call(
        functools.partial(score_kernel, query_parts, key_parts, len(blocks), first, last),
        out_shape=shapes,
        compiler_params=pltpu.CompilerParams(vmem_limit_bytes=32 * 1024 * 1024),
        cost_estimate=pl.CostEstimate(
            flops=2 * count * key_rows * width,
            bytes_accessed=2 * width * (count + key_rows),
            transcendentals=0,
        ),
        name="score",
    )(*blocks, *(() if first else state))
    if last:
        return result
    return result if first else (result, state[1])


def per_device(embeddings, cluster_id):
    ny, nz, nx = 4, 4, 4

    def place(y, z, x, core):
        return (((y % ny) * nz + z % nz) * nx + x % nx) * 2 + core

    def fetch(value, *offsets):
        pairs = []
        for y in range(ny):
            for z in range(nz):
                for x in range(nx):
                    for core, (dy, dz, dx) in enumerate(offsets):
                        pairs.append((place(y + dy, z + dz, x + dx, core), place(y, z, x, core)))
        return lax.ppermute(value, AXES, pairs)

    def give(value, *offsets):
        return fetch(value, *(tuple(-o for o in offset) for offset in offsets))

    def swap(value):
        return lax.ppermute(value, AXES, [(i, i ^ 1) for i in range(ny * nz * nx * 2)])

    block, half = pack(embeddings, swap(embeddings), cluster_id, swap(cluster_id))

    key1 = fetch(block, (0, 0, 1), (0, 1, 0))
    key2 = fetch(block, (0, 0, -1), (0, -1, 0))
    near = fetch(block, (1, 0, 0), (-1, 0, 0))
    far = fetch(half, (2, 0, 0), (2, 0, 0))
    key4 = fetch(key1, (0, 1, 0), (0, 0, -1))
    key5 = fetch(key2, (0, -1, 0), (0, 0, 1))
    key3 = fetch(key1, (0, 0, 1), (0, 1, 0))
    key6 = fetch(key4, (0, 1, 0), (0, 0, -1))
    key7 = fetch(key5, (0, -1, 0), (0, 0, 1))
    key8 = fetch(key7[:HALF], (0, 0, -1), (0, -1, 0))

    queries = [(block, (OWN,)), whole(far), whole(near), (block, (OTHER,)), whole(swap(far)), whole(swap(near))]
    state = score(queries, [(block, (OWN,)), whole(key1), whole(key2)])
    state = score(queries, [whole(key4), whole(key5)], state)
    state = score(queries, [whole(key3)], state)
    state = score(queries, [whole(key6), whole(key7)], state)
    best = score(queries, [whole(key8)], state, last=True)[0]
    best = jnp.maximum(best[: 4 * ROWS], swap(best[4 * ROWS :]))

    from_far = give(best[ROWS : 2 * ROWS], (2, 0, 0), (2, 0, 0))
    from_near = give(best[2 * ROWS :], (1, 0, 0), (-1, 0, 0))
    mine = jnp.maximum(best[:ROWS], jnp.maximum(from_far, from_near[:ROWS]))
    return jnp.maximum(mine, swap(from_near[ROWS:]))


def solution(mesh):
    in_specs = (P(AXES, None), P(AXES))
    return jax.shard_map(
        per_device, mesh=mesh, in_specs=in_specs, out_specs=P(AXES), check_vma=False
    )
```

```python
import functools

import jax
import jax.numpy as jnp
from jax import lax
from jax.experimental import pallas as pl
from jax.experimental.pallas import tpu as pltpu
from jax.sharding import PartitionSpec as P

AXES = ("grp", "dev")
ROWS = 256
TAIL = 16
HALF = ROWS + TAIL
BLOCK = HALF + ROWS
SECOND = HALF
LANES = 128
FLOOR = -1.0


def unit(rows):
    values = rows.astype(jnp.float32)
    norm = jnp.sqrt(jnp.sum(values * values, axis=1, keepdims=True) + 1e-06)
    return (values / norm).astype(jnp.bfloat16)


def spread(ids):
    return jnp.broadcast_to(ids.astype(jnp.float32), (TAIL, ROWS)).astype(jnp.bfloat16)


def own_kernel(rows_ref, ids_ref, half_ref):
    half_ref[0:ROWS, :] = unit(rows_ref[...])
    half_ref[ROWS:HALF, 0:ROWS] = spread(ids_ref[...])
    half_ref[ROWS:HALF, ROWS:] = jnp.zeros((TAIL, half_ref.shape[1] - ROWS), jnp.bfloat16)


def chip_kernel(half_ref, rows_ref, ids_ref, block_ref):
    block_ref[0:HALF, :] = half_ref[...]
    block_ref[ROWS:HALF, ROWS : 2 * ROWS] = spread(ids_ref[...])
    block_ref[SECOND:BLOCK, :] = unit(rows_ref[...])


def call(kernel, name, rows, width, *operands):
    return pl.pallas_call(
        kernel,
        out_shape=jax.ShapeDtypeStruct((rows, width), jnp.bfloat16),
        compiler_params=pltpu.CompilerParams(vmem_limit_bytes=16 * 1024 * 1024),
        name=name,
    )(*operands)


OWN, OTHER = (0, 0), (SECOND, ROWS)


def whole(block):
    return (block, (OWN,) if block.shape[0] == HALF else (OWN, OTHER))


def ids_row(ref, lane):
    return ref[ROWS:HALF, lane : lane + ROWS].astype(jnp.float32)[0:1, :]


def score_kernel(groups, key_parts, n_blocks, first, last, collect, *refs):
    blocks, refs = refs[:n_blocks], list(refs[n_blocks:])
    key_parts = [(blocks[at], row, lane) for at, (row, lane) in key_parts]
    row_index = lax.broadcasted_iota(jnp.int32, (ROWS, ROWS), 0)
    col_index = lax.broadcasted_iota(jnp.int32, (ROWS, ROWS), 1)
    states = [(None, None) if first else (refs.pop(0), refs.pop(0)) for _ in groups]
    results = [(refs.pop(0), refs.pop(0) if first else column_ref) for _, column_ref in states]
    tops = {}
    for group, (query_parts, own_key) in enumerate(groups):
        before_ref, (best_ref, column_ref) = states[group][0], results[group]
        for place, (at, (row, lane)) in enumerate(query_parts):
            here = slice(place * ROWS, (place + 1) * ROWS)
            rows = blocks[at][row : row + ROWS, :]
            if first:
                ids = jnp.broadcast_to(ids_row(blocks[at], lane), (ROWS, ROWS))
                column = jnp.sum(jnp.where(row_index == col_index, ids, 0.0), axis=1, keepdims=True)
                column = jnp.broadcast_to(column, (ROWS, LANES))
                column_ref[here, :] = column
                best = jnp.full((ROWS, LANES), FLOOR, jnp.float32)
            else:
                column, best = column_ref[here, :], before_ref[here, :]
            for number, (key_ref, key_row, key_lane) in enumerate(key_parts):
                scores = lax.dot_general(
                    rows,
                    key_ref[key_row : key_row + ROWS, :],
                    (((1,), (1,)), ((), ())),
                    preferred_element_type=jnp.float32,
                )
                ids = ids_row(key_ref, key_lane)
                for start in range(0, ROWS, LANES):
                    lanes = slice(start, start + LANES)
                    match = column == ids[:, lanes]
                    if own_key and place == 0 and number == 0:
                        match = match & (row_index[:, lanes] != col_index[:, lanes])
                    kept = jnp.where(match, scores[:, lanes], FLOOR)
                    best = jnp.maximum(best, kept)
                    if number >= collect:
                        top = jnp.max(kept.reshape(ROWS // 8, 8, LANES), axis=0)
                        at_top = (number, start)
                        tops[at_top] = jnp.maximum(tops[at_top], top) if at_top in tops else top
            if last:
                best_ref[0:1, here] = jnp.max(best.T, axis=0, keepdims=True)
            else:
                best_ref[here, :] = best
    for (number, start), top in tops.items():
        at = (number - collect) * ROWS + start
        refs[0][0:1, at : at + LANES] = jnp.max(top, axis=0, keepdims=True)


def score(groups, keys, states=None, last=False, collect=None, own_key=False):
    blocks = []

    def listed(pieces):
        found = []
        for block, parts in pieces:
            at = next((i for i, b in enumerate(blocks) if b is block), len(blocks))
            if at == len(blocks):
                blocks.append(block)
            found += [(at, part) for part in parts]
        return found

    listed_groups = [(listed(group), own_key and i == 0) for i, group in enumerate(groups)]
    key_parts = listed(keys)
    counts = [len(parts) * ROWS for parts, _ in listed_groups]
    count, key_rows, width = sum(counts), len(key_parts) * ROWS, blocks[0].shape[1]
    skipped = len(key_parts) if collect is None else sum(len(parts) for _, parts in keys[:collect])
    first = states is None
    shapes = []
    for rows in counts:
        wide = jax.ShapeDtypeStruct((rows, LANES), jnp.float32)
        shapes.append(jax.ShapeDtypeStruct((1, rows), jnp.float32) if last else wide)
        if first:
            shapes.append(wide)
    if collect is not None:
        shapes.append(jax.ShapeDtypeStruct((1, key_rows - skipped * ROWS), jnp.float32))
    result = pl.pallas_call(
        functools.partial(score_kernel, listed_groups, key_parts, len(blocks), first, last, skipped),
        out_shape=tuple(shapes),
        compiler_params=pltpu.CompilerParams(vmem_limit_bytes=32 * 1024 * 1024),
        cost_estimate=pl.CostEstimate(
            flops=2 * count * key_rows * width,
            bytes_accessed=2 * width * (count + key_rows),
            transcendentals=0,
        ),
        name="score",
    )(*blocks, *(() if first else (x for state in states for x in state)))
    if first:
        states = [(result[2 * i], result[2 * i + 1]) for i in range(len(groups))]
    else:
        states = [(result[i], states[i][1]) for i in range(len(groups))]
    return states, (None if collect is None else result[-1][0])


def per_device(embeddings, cluster_id):
    ny, nz, nx = 4, 4, 4

    def place(y, z, x, core):
        return (((y % ny) * nz + z % nz) * nx + x % nx) * 2 + core

    def fetch(value, *offsets):
        pairs = []
        for y in range(ny):
            for z in range(nz):
                for x in range(nx):
                    for core, (dy, dz, dx) in enumerate(offsets):
                        pairs.append((place(y + dy, z + dz, x + dx, core), place(y, z, x, core)))
        return lax.ppermute(value, AXES, pairs)

    def give(value, *offsets):
        return fetch(value, *(tuple(-o for o in offset) for offset in offsets))

    def swap(value):
        return lax.ppermute(value, AXES, [(i, i ^ 1) for i in range(ny * nz * nx * 2)])

    width = embeddings.shape[1]
    ids = cluster_id.reshape(1, ROWS)
    half = call(own_kernel, "own", HALF, width, embeddings, ids)
    block = call(chip_kernel, "chip", BLOCK, width, half, swap(embeddings), swap(cluster_id).reshape(1, ROWS))

    key1 = fetch(block, (0, 0, 1), (0, 1, 0))
    key2 = fetch(block, (0, 0, 2), (0, 2, 0))
    near = fetch(block, (1, 0, 0), (-1, 0, 0))
    far = fetch(half, (2, 0, 0), (2, 0, 0))
    key3 = fetch(key1, (0, 1, 0), (0, 0, -1))
    key4 = fetch(key2, (0, -1, 0), (0, 0, 1))
    key5 = fetch(key2[:HALF], (0, 2, 0), (0, 0, 2))

    groups = [[(block, (OWN, OTHER))], [whole(near), (swap(near), (OTHER, OWN)), whole(far), whole(swap(far))]]
    keys = [(block, (OWN,)), whole(key1), whole(key2)]
    states, top1 = score(groups, keys, collect=1, own_key=True)
    states, top4 = score(groups, [whole(key4)], states, collect=0)
    states, top3 = score(groups, [whole(key3)], states, collect=0)
    (best, best2), _ = score(groups, [whole(key5)], states, last=True)
    best, best2 = best[0].reshape(1, 2 * ROWS), best2[0].reshape(3, 2 * ROWS)
    best, best2 = [best[0], best2[0], best2[1]], best2[2]
    homes = [give(top1[: 2 * ROWS], (0, 0, 1), (0, 1, 0)), give(top3, (0, 1, 1), (0, 1, -1)), give(top4, (0, -1, 2), (0, 2, 1))]

    from_far = give(best2, (2, 0, 0), (2, 0, 0))
    from_up = give(best[1], (1, 0, 0), (-1, 0, 0))
    from_down = give(best[2], (-1, 0, 0), (1, 0, 0))
    home = functools.reduce(jnp.maximum, [best[0], *homes, from_far, from_up, from_down])
    return jnp.maximum(home[:ROWS], swap(home[ROWS:]))


def solution(mesh):
    in_specs = (P(AXES, None), P(AXES))
    return jax.shard_map(
        per_device, mesh=mesh, in_specs=in_specs, out_specs=P(AXES), check_vma=False
    )
```

```python
import functools

import jax
import jax.numpy as jnp
from jax import lax
from jax.experimental import pallas as pl
from jax.experimental.pallas import tpu as pltpu
from jax.sharding import PartitionSpec as P

AXES = ("grp", "dev")
ROWS = 256
TAIL = 16
HALF = ROWS + TAIL
BLOCK = HALF + ROWS
SECOND = HALF
LANES = 128
FLOOR = -1.0


def unit(rows):
    values = rows.astype(jnp.float32)
    norm = jnp.sqrt(jnp.sum(values * values, axis=1, keepdims=True) + 1e-06)
    return (values / norm).astype(jnp.bfloat16)


def spread(ids):
    return jnp.broadcast_to(ids.astype(jnp.float32), (TAIL, ROWS)).astype(jnp.bfloat16)


def own_kernel(rows_ref, ids_ref, half_ref):
    half_ref[0:ROWS, :] = unit(rows_ref[...])
    half_ref[ROWS:HALF, 0:ROWS] = spread(ids_ref[...])
    half_ref[ROWS:HALF, ROWS:] = jnp.zeros((TAIL, half_ref.shape[1] - ROWS), jnp.bfloat16)


def chip_kernel(half_ref, rows_ref, ids_ref, block_ref):
    block_ref[0:HALF, :] = half_ref[...]
    block_ref[ROWS:HALF, ROWS : 2 * ROWS] = spread(ids_ref[...])
    block_ref[SECOND:BLOCK, :] = unit(rows_ref[...])


def call(kernel, name, rows, width, *operands):
    return pl.pallas_call(
        kernel,
        out_shape=jax.ShapeDtypeStruct((rows, width), jnp.bfloat16),
        compiler_params=pltpu.CompilerParams(vmem_limit_bytes=16 * 1024 * 1024),
        name=name,
    )(*operands)


OWN, OTHER = (0, 0), (SECOND, ROWS)


def whole(block):
    return (block, (OWN,) if block.shape[0] == HALF else (OWN, OTHER))


def ids_row(ref, lane):
    return ref[ROWS:HALF, lane : lane + ROWS].astype(jnp.float32)[0:1, :]


def score_kernel(groups, key_parts, n_blocks, first, last, collect, *refs):
    blocks, refs = refs[:n_blocks], list(refs[n_blocks:])
    key_parts = [(blocks[at], row, lane) for at, (row, lane) in key_parts]
    row_index = lax.broadcasted_iota(jnp.int32, (ROWS, ROWS), 0)
    col_index = lax.broadcasted_iota(jnp.int32, (ROWS, ROWS), 1)
    states = [(None, None) if first else (refs.pop(0), refs.pop(0)) for _ in groups]
    results = [(refs.pop(0), refs.pop(0) if first else column_ref) for _, column_ref in states]
    tops = {}
    for group, (query_parts, own_key) in enumerate(groups):
        before_ref, (best_ref, column_ref) = states[group][0], results[group]
        for place, (at, (row, lane)) in enumerate(query_parts):
            here = slice(place * ROWS, (place + 1) * ROWS)
            rows = blocks[at][row : row + ROWS, :]
            if first:
                ids = jnp.broadcast_to(ids_row(blocks[at], lane), (ROWS, ROWS))
                column = jnp.sum(jnp.where(row_index == col_index, ids, 0.0), axis=1, keepdims=True)
                column = jnp.broadcast_to(column, (ROWS, LANES))
                column_ref[here, :] = column
                best = jnp.full((ROWS, LANES), FLOOR, jnp.float32)
            else:
                column, best = column_ref[here, :], before_ref[here, :]
            for number, (key_ref, key_row, key_lane) in enumerate(key_parts):
                scores = lax.dot_general(
                    rows,
                    key_ref[key_row : key_row + ROWS, :],
                    (((1,), (1,)), ((), ())),
                    preferred_element_type=jnp.float32,
                )
                ids = ids_row(key_ref, key_lane)
                for start in range(0, ROWS, LANES):
                    lanes = slice(start, start + LANES)
                    match = column == ids[:, lanes]
                    if own_key and place == 0 and number == 0:
                        match = match & (row_index[:, lanes] != col_index[:, lanes])
                    kept = jnp.where(match, scores[:, lanes], FLOOR)
                    best = jnp.maximum(best, kept)
                    if number >= collect:
                        top = jnp.max(kept.reshape(ROWS // 8, 8, LANES), axis=0)
                        at_top = (number, start)
                        tops[at_top] = jnp.maximum(tops[at_top], top) if at_top in tops else top
            if last:
                best_ref[0:1, here] = jnp.max(best.T, axis=0, keepdims=True)
            else:
                best_ref[here, :] = best
    for (number, start), top in tops.items():
        at = (number - collect) * ROWS + start
        refs[0][0:1, at : at + LANES] = jnp.max(top, axis=0, keepdims=True)


def score(groups, keys, states=None, last=False, collect=None, own_key=False):
    blocks = []

    def listed(pieces):
        found = []
        for block, parts in pieces:
            at = next((i for i, b in enumerate(blocks) if b is block), len(blocks))
            if at == len(blocks):
                blocks.append(block)
            found += [(at, part) for part in parts]
        return found

    listed_groups = [(listed(group), own_key and i == 0) for i, group in enumerate(groups)]
    key_parts = listed(keys)
    counts = [len(parts) * ROWS for parts, _ in listed_groups]
    count, key_rows, width = sum(counts), len(key_parts) * ROWS, blocks[0].shape[1]
    skipped = len(key_parts) if collect is None else sum(len(parts) for _, parts in keys[:collect])
    first = states is None
    shapes = []
    for rows in counts:
        wide = jax.ShapeDtypeStruct((rows, LANES), jnp.float32)
        shapes.append(jax.ShapeDtypeStruct((1, rows), jnp.float32) if last else wide)
        if first:
            shapes.append(wide)
    if collect is not None:
        shapes.append(jax.ShapeDtypeStruct((1, key_rows - skipped * ROWS), jnp.float32))
    result = pl.pallas_call(
        functools.partial(score_kernel, listed_groups, key_parts, len(blocks), first, last, skipped),
        out_shape=tuple(shapes),
        compiler_params=pltpu.CompilerParams(vmem_limit_bytes=32 * 1024 * 1024),
        cost_estimate=pl.CostEstimate(
            flops=2 * count * key_rows * width,
            bytes_accessed=2 * width * (count + key_rows),
            transcendentals=0,
        ),
        name="score",
    )(*blocks, *(() if first else (x for state in states for x in state)))
    if first:
        states = [(result[2 * i], result[2 * i + 1]) for i in range(len(groups))]
    else:
        states = [(result[i], states[i][1]) for i in range(len(groups))]
    return states, (None if collect is None else result[-1][0])


def per_device(embeddings, cluster_id):
    ny, nz, nx = 4, 4, 4

    def place(y, z, x, core):
        return (((y % ny) * nz + z % nz) * nx + x % nx) * 2 + core

    def fetch(value, *offsets):
        pairs = []
        for y in range(ny):
            for z in range(nz):
                for x in range(nx):
                    for core, (dy, dz, dx) in enumerate(offsets):
                        pairs.append((place(y + dy, z + dz, x + dx, core), place(y, z, x, core)))
        return lax.ppermute(value, AXES, pairs)

    def give(value, *offsets):
        return fetch(value, *(tuple(-o for o in offset) for offset in offsets))

    def swap(value):
        return lax.ppermute(value, AXES, [(i, i ^ 1) for i in range(ny * nz * nx * 2)])

    width = embeddings.shape[1]
    ids = cluster_id.reshape(1, ROWS)
    half = call(own_kernel, "own", HALF, width, embeddings, ids)
    block = call(chip_kernel, "chip", BLOCK, width, half, swap(embeddings), swap(cluster_id).reshape(1, ROWS))

    after = lax.optimization_barrier

    key1 = fetch(block, (0, 0, 1), (0, 1, 0))
    key2 = fetch(block, (0, 0, 2), (0, 2, 0))
    near = fetch(block, (1, 0, 0), (-1, 0, 0))
    key4 = fetch(key2, (0, -1, 0), (0, 0, -1))
    key3 = fetch(key1, (0, -1, 0), (0, 0, 1))
    far = fetch(near, (1, 0, 0), (-1, 0, 0))
    key5 = fetch(key2[:HALF], (0, 2, 0), (0, 0, 2))

    keys = [(block, (OWN,)), whole(key1), whole(key2)]
    first = [(block, (OWN, OTHER)), whole(near), (swap(near), (OTHER, OWN))]
    (state,), top = score([first], keys, collect=1, own_key=True)
    far, state = after((far, state))
    second = [whole(far)]
    (state2,), top2 = score([second], keys, collect=1)
    groups, states = [first, second], [state, state2]
    home1 = give(jnp.maximum(top, top2)[: 2 * ROWS], (0, 0, 1), (0, 1, 0))
    states, top4 = score(groups, [whole(key4)], states, collect=0)
    home4 = give(top4, (0, -1, 2), (0, 2, -1))
    states, top3 = score(groups, [whole(key3)], states, collect=0)
    home3 = give(top3, (0, -1, 1), (0, 1, 1))
    key5, home1, home4 = after((key5, home1, home4))
    (best, best2), _ = score(groups, [whole(key5)], states, last=True)
    best, best2 = best[0].reshape(3, 2 * ROWS), best2[0][0]
    from_far = give(best2, (2, 0, 0), (2, 0, 0))
    from_up = give(best[1], (1, 0, 0), (-1, 0, 0))
    from_down = give(best[2], (-1, 0, 0), (1, 0, 0))
    home = functools.reduce(jnp.maximum, [best[0], home1, home4, home3, from_far, from_up, from_down])
    return jnp.maximum(home[:ROWS], swap(home[ROWS:]))


def solution(mesh):
    in_specs = (P(AXES, None), P(AXES))
    return jax.shard_map(
        per_device, mesh=mesh, in_specs=in_specs, out_specs=P(AXES), check_vma=False
    )
```

```python
import functools

import jax
import jax.numpy as jnp
from jax import lax
from jax.experimental import pallas as pl
from jax.experimental.pallas import tpu as pltpu
from jax.sharding import PartitionSpec as P

AXES = ("grp", "dev")
ROWS = 256
TAIL = 16
HALF = ROWS + TAIL
BLOCK = HALF + ROWS
SECOND = HALF
LANES = 128
FLOOR = -1.0


def unit(rows):
    values = rows.astype(jnp.float32)
    norm = jnp.sqrt(jnp.sum(values * values, axis=1, keepdims=True) + 1e-06)
    return (values / norm).astype(jnp.bfloat16)


def spread(ids):
    return jnp.broadcast_to(ids.astype(jnp.float32), (TAIL, ROWS)).astype(jnp.bfloat16)


def own_kernel(rows_ref, ids_ref, half_ref):
    half_ref[0:ROWS, :] = unit(rows_ref[...])
    half_ref[ROWS:HALF, 0:ROWS] = spread(ids_ref[...])
    half_ref[ROWS:HALF, ROWS:] = jnp.zeros((TAIL, half_ref.shape[1] - ROWS), jnp.bfloat16)


def chip_kernel(half_ref, rows_ref, ids_ref, block_ref):
    block_ref[0:HALF, :] = half_ref[...]
    block_ref[ROWS:HALF, ROWS : 2 * ROWS] = spread(ids_ref[...])
    block_ref[SECOND:BLOCK, :] = unit(rows_ref[...])


def call(kernel, name, rows, width, *operands):
    return pl.pallas_call(
        kernel,
        out_shape=jax.ShapeDtypeStruct((rows, width), jnp.bfloat16),
        compiler_params=pltpu.CompilerParams(vmem_limit_bytes=16 * 1024 * 1024),
        name=name,
    )(*operands)


OWN, OTHER = (0, 0), (SECOND, ROWS)


def whole(block):
    return (block, (OWN,) if block.shape[0] == HALF else (OWN, OTHER))


def ids_row(ref, lane):
    return ref[ROWS:HALF, lane : lane + ROWS].astype(jnp.float32)[0:1, :]


def score_kernel(groups, key_parts, n_blocks, first, last, collect, *refs):
    blocks, refs = refs[:n_blocks], list(refs[n_blocks:])
    key_parts = [(blocks[at], row, lane) for at, (row, lane) in key_parts]
    row_index = lax.broadcasted_iota(jnp.int32, (ROWS, ROWS), 0)
    col_index = lax.broadcasted_iota(jnp.int32, (ROWS, ROWS), 1)
    states = [(None, None) if first else (refs.pop(0), refs.pop(0)) for _ in groups]
    results = [(refs.pop(0), refs.pop(0) if first else column_ref) for _, column_ref in states]
    tops = {}
    for group, (query_parts, own_key) in enumerate(groups):
        before_ref, (best_ref, column_ref) = states[group][0], results[group]
        for place, (at, (row, lane)) in enumerate(query_parts):
            here = slice(place * ROWS, (place + 1) * ROWS)
            rows = blocks[at][row : row + ROWS, :]
            if first:
                ids = jnp.broadcast_to(ids_row(blocks[at], lane), (ROWS, ROWS))
                column = jnp.sum(jnp.where(row_index == col_index, ids, 0.0), axis=1, keepdims=True)
                column = jnp.broadcast_to(column, (ROWS, LANES))
                column_ref[here, :] = column
                best = jnp.full((ROWS, LANES), FLOOR, jnp.float32)
            else:
                column, best = column_ref[here, :], before_ref[here, :]
            for number, (key_ref, key_row, key_lane) in enumerate(key_parts):
                scores = lax.dot_general(
                    rows,
                    key_ref[key_row : key_row + ROWS, :],
                    (((1,), (1,)), ((), ())),
                    preferred_element_type=jnp.float32,
                )
                ids = ids_row(key_ref, key_lane)
                for start in range(0, ROWS, LANES):
                    lanes = slice(start, start + LANES)
                    match = column == ids[:, lanes]
                    if own_key and place == 0 and number == 0:
                        match = match & (row_index[:, lanes] != col_index[:, lanes])
                    kept = jnp.where(match, scores[:, lanes], FLOOR)
                    best = jnp.maximum(best, kept)
                    if number >= collect:
                        top = jnp.max(kept.reshape(ROWS // 8, 8, LANES), axis=0)
                        at_top = (number, start)
                        tops[at_top] = jnp.maximum(tops[at_top], top) if at_top in tops else top
            if last:
                best_ref[0:1, here] = jnp.max(best.T, axis=0, keepdims=True)
            else:
                best_ref[here, :] = best
    for (number, start), top in tops.items():
        at = (number - collect) * ROWS + start
        refs[0][0:1, at : at + LANES] = jnp.max(top, axis=0, keepdims=True)


def score(groups, keys, states=None, last=False, collect=None, own_key=False):
    blocks = []

    def listed(pieces):
        found = []
        for block, parts in pieces:
            at = next((i for i, b in enumerate(blocks) if b is block), len(blocks))
            if at == len(blocks):
                blocks.append(block)
            found += [(at, part) for part in parts]
        return found

    listed_groups = [(listed(group), own_key and i == 0) for i, group in enumerate(groups)]
    key_parts = listed(keys)
    counts = [len(parts) * ROWS for parts, _ in listed_groups]
    count, key_rows, width = sum(counts), len(key_parts) * ROWS, blocks[0].shape[1]
    skipped = len(key_parts) if collect is None else sum(len(parts) for _, parts in keys[:collect])
    first = states is None
    shapes = []
    for rows in counts:
        wide = jax.ShapeDtypeStruct((rows, LANES), jnp.float32)
        shapes.append(jax.ShapeDtypeStruct((1, rows), jnp.float32) if last else wide)
        if first:
            shapes.append(wide)
    if collect is not None:
        shapes.append(jax.ShapeDtypeStruct((1, key_rows - skipped * ROWS), jnp.float32))
    result = pl.pallas_call(
        functools.partial(score_kernel, listed_groups, key_parts, len(blocks), first, last, skipped),
        out_shape=tuple(shapes),
        compiler_params=pltpu.CompilerParams(vmem_limit_bytes=32 * 1024 * 1024),
        cost_estimate=pl.CostEstimate(
            flops=2 * count * key_rows * width,
            bytes_accessed=2 * width * (count + key_rows),
            transcendentals=0,
        ),
        name="score",
    )(*blocks, *(() if first else (x for state in states for x in state)))
    if first:
        states = [(result[2 * i], result[2 * i + 1]) for i in range(len(groups))]
    else:
        states = [(result[i], states[i][1]) for i in range(len(groups))]
    return states, (None if collect is None else result[-1][0])


def per_device(embeddings, cluster_id):
    ny, nz, nx = 4, 4, 4

    def place(y, z, x, core):
        return (((y % ny) * nz + z % nz) * nx + x % nx) * 2 + core

    def fetch(value, *offsets):
        pairs = []
        for y in range(ny):
            for z in range(nz):
                for x in range(nx):
                    for core, (dy, dz, dx) in enumerate(offsets):
                        pairs.append((place(y + dy, z + dz, x + dx, core), place(y, z, x, core)))
        return lax.ppermute(value, AXES, pairs)

    def give(value, *offsets):
        return fetch(value, *(tuple(-o for o in offset) for offset in offsets))

    def swap(value):
        return lax.ppermute(value, AXES, [(i, i ^ 1) for i in range(ny * nz * nx * 2)])

    width = embeddings.shape[1]
    ids = cluster_id.reshape(1, ROWS)
    half = call(own_kernel, "own", HALF, width, embeddings, ids)
    block = call(chip_kernel, "chip", BLOCK, width, half, swap(embeddings), swap(cluster_id).reshape(1, ROWS))

    after = lax.optimization_barrier

    key1 = fetch(block, (0, 0, 1), (0, 1, 0))
    key2 = fetch(block, (0, 0, 2), (0, 2, 0))
    near = fetch(block, (1, 0, 0), (-1, 0, 0))
    key4 = fetch(key2, (0, -1, 0), (0, 0, -1))
    far = fetch(near, (1, 0, 0), (-1, 0, 0))

    first = [(block, (OWN, OTHER)), whole(near), (swap(near), (OTHER, OWN))]
    second = [whole(far)]
    (state,), _ = score([first], [(block, (OWN,)), whole(key2)], own_key=True)
    key3 = fetch(key1, (0, -1, 0), (0, 0, 1))
    (state,), top1 = score([first], [whole(key1)], [state], collect=0)
    key4, state = after((key4, state))
    key5 = fetch(key4[:HALF], (0, -1, 0), (0, 0, -1))
    (state,), top4 = score([first], [whole(key4)], [state], collect=0)
    far, state = after((far, state))
    (state2,), tops = score([second], [(block, (OWN,)), whole(key2), whole(key1), whole(key4)], collect=2)
    home1 = give(jnp.maximum(top1, tops[: 2 * ROWS]), (0, 0, 1), (0, 1, 0))
    home4 = give(jnp.maximum(top4, tops[2 * ROWS :]), (0, -1, 2), (0, 2, -1))
    (state, state2), top3 = score([first, second], [whole(key3)], [state, state2], collect=0)
    home3 = give(top3, (0, -1, 1), (0, 1, 1))
    ((best2, _),), _ = score([second], [whole(key5)], [state2], last=True)
    ((best, _),), _ = score([first], [whole(key5)], [state], last=True)
    best = best[0].reshape(3, 2 * ROWS)

    from_far = give(best2[0], (2, 0, 0), (2, 0, 0))
    from_up = give(best[1], (1, 0, 0), (-1, 0, 0))
    from_down = give(best[2], (-1, 0, 0), (1, 0, 0))
    home = functools.reduce(jnp.maximum, [best[0], home1, home4, home3, from_far, from_up, from_down])
    return jnp.maximum(home[:ROWS], swap(home[ROWS:]))


def solution(mesh):
    in_specs = (P(AXES, None), P(AXES))
    return jax.shard_map(
        per_device, mesh=mesh, in_specs=in_specs, out_specs=P(AXES), check_vma=False
    )
```

```python
import functools

import jax
import jax.numpy as jnp
from jax import lax
from jax.experimental import pallas as pl
from jax.experimental.pallas import tpu as pltpu
from jax.sharding import PartitionSpec as P

AXES = ("grp", "dev")
ROWS = 256
TAIL = 16
HALF = ROWS + TAIL
BLOCK = HALF + ROWS
SECOND = HALF
LANES = 128
FLOOR = -1.0


def unit(rows):
    values = rows.astype(jnp.float32)
    norm = jnp.sqrt(jnp.sum(values * values, axis=1, keepdims=True) + 1e-06)
    return (values / norm).astype(jnp.bfloat16)


def spread(ids):
    return jnp.broadcast_to(ids.astype(jnp.float32), (TAIL, ROWS)).astype(jnp.bfloat16)


def own_kernel(rows_ref, ids_ref, half_ref):
    half_ref[0:ROWS, :] = unit(rows_ref[...])
    half_ref[ROWS:HALF, 0:ROWS] = spread(ids_ref[...])
    half_ref[ROWS:HALF, ROWS:] = jnp.zeros((TAIL, half_ref.shape[1] - ROWS), jnp.bfloat16)


def chip_kernel(half_ref, rows_ref, ids_ref, block_ref):
    block_ref[0:HALF, :] = half_ref[...]
    block_ref[ROWS:HALF, ROWS : 2 * ROWS] = spread(ids_ref[...])
    block_ref[SECOND:BLOCK, :] = unit(rows_ref[...])


def call(kernel, name, rows, width, *operands):
    return pl.pallas_call(
        kernel,
        out_shape=jax.ShapeDtypeStruct((rows, width), jnp.bfloat16),
        compiler_params=pltpu.CompilerParams(vmem_limit_bytes=16 * 1024 * 1024),
        name=name,
    )(*operands)


OWN, OTHER = (0, 0), (SECOND, ROWS)


def whole(block):
    return (block, (OWN,) if block.shape[0] == HALF else (OWN, OTHER))


def ids_row(ref, lane):
    return ref[ROWS:HALF, lane : lane + ROWS].astype(jnp.float32)[0:1, :]


def score_kernel(groups, key_parts, n_blocks, first, last, collect, *refs):
    blocks, refs = refs[:n_blocks], list(refs[n_blocks:])
    key_parts = [(blocks[at], row, lane) for at, (row, lane) in key_parts]
    row_index = lax.broadcasted_iota(jnp.int32, (ROWS, ROWS), 0)
    col_index = lax.broadcasted_iota(jnp.int32, (ROWS, ROWS), 1)
    states = [(None, None) if first else (refs.pop(0), refs.pop(0)) for _ in groups]
    results = [(refs.pop(0), refs.pop(0) if first else column_ref) for _, column_ref in states]
    tops = {}
    for group, (query_parts, own_key) in enumerate(groups):
        before_ref, (best_ref, column_ref) = states[group][0], results[group]
        for place, (at, (row, lane)) in enumerate(query_parts):
            here = slice(place * ROWS, (place + 1) * ROWS)
            rows = blocks[at][row : row + ROWS, :]
            if first:
                ids = jnp.broadcast_to(ids_row(blocks[at], lane), (ROWS, ROWS))
                column = jnp.sum(jnp.where(row_index == col_index, ids, 0.0), axis=1, keepdims=True)
                column = jnp.broadcast_to(column, (ROWS, LANES))
                column_ref[here, :] = column
                best = jnp.full((ROWS, LANES), FLOOR, jnp.float32)
            else:
                column, best = column_ref[here, :], before_ref[here, :]
            for number, (key_ref, key_row, key_lane) in enumerate(key_parts):
                scores = lax.dot_general(
                    rows,
                    key_ref[key_row : key_row + ROWS, :],
                    (((1,), (1,)), ((), ())),
                    preferred_element_type=jnp.float32,
                )
                ids = ids_row(key_ref, key_lane)
                for start in range(0, ROWS, LANES):
                    lanes = slice(start, start + LANES)
                    match = column == ids[:, lanes]
                    if own_key and place == 0 and number == 0:
                        match = match & (row_index[:, lanes] != col_index[:, lanes])
                    kept = jnp.where(match, scores[:, lanes], FLOOR)
                    best = jnp.maximum(best, kept)
                    if number >= collect:
                        top = jnp.max(kept.reshape(ROWS // 8, 8, LANES), axis=0)
                        at_top = (number, start)
                        tops[at_top] = jnp.maximum(tops[at_top], top) if at_top in tops else top
            if last:
                best_ref[0:1, here] = jnp.max(best.T, axis=0, keepdims=True)
            else:
                best_ref[here, :] = best
    for (number, start), top in tops.items():
        at = (number - collect) * ROWS + start
        refs[0][0:1, at : at + LANES] = jnp.max(top, axis=0, keepdims=True)


def score(groups, keys, states=None, last=False, collect=None, own_key=False):
    blocks = []

    def listed(pieces):
        found = []
        for block, parts in pieces:
            at = next((i for i, b in enumerate(blocks) if b is block), len(blocks))
            if at == len(blocks):
                blocks.append(block)
            found += [(at, part) for part in parts]
        return found

    listed_groups = [(listed(group), own_key and i == 0) for i, group in enumerate(groups)]
    key_parts = listed(keys)
    counts = [len(parts) * ROWS for parts, _ in listed_groups]
    count, key_rows, width = sum(counts), len(key_parts) * ROWS, blocks[0].shape[1]
    skipped = len(key_parts) if collect is None else sum(len(parts) for _, parts in keys[:collect])
    first = states is None
    shapes = []
    for rows in counts:
        wide = jax.ShapeDtypeStruct((rows, LANES), jnp.float32)
        shapes.append(jax.ShapeDtypeStruct((1, rows), jnp.float32) if last else wide)
        if first:
            shapes.append(wide)
    if collect is not None:
        shapes.append(jax.ShapeDtypeStruct((1, key_rows - skipped * ROWS), jnp.float32))
    result = pl.pallas_call(
        functools.partial(score_kernel, listed_groups, key_parts, len(blocks), first, last, skipped),
        out_shape=tuple(shapes),
        compiler_params=pltpu.CompilerParams(vmem_limit_bytes=32 * 1024 * 1024),
        cost_estimate=pl.CostEstimate(
            flops=2 * count * key_rows * width,
            bytes_accessed=2 * width * (count + key_rows),
            transcendentals=0,
        ),
        name="score",
    )(*blocks, *(() if first else (x for state in states for x in state)))
    if first:
        states = [(result[2 * i], result[2 * i + 1]) for i in range(len(groups))]
    else:
        states = [(result[i], states[i][1]) for i in range(len(groups))]
    return states, (None if collect is None else result[-1][0])


def per_device(embeddings, cluster_id):
    ny, nz, nx = 4, 4, 4

    def place(y, z, x, core):
        return (((y % ny) * nz + z % nz) * nx + x % nx) * 2 + core

    def fetch(value, *offsets):
        pairs = []
        for y in range(ny):
            for z in range(nz):
                for x in range(nx):
                    for core, (dy, dz, dx) in enumerate(offsets):
                        pairs.append((place(y + dy, z + dz, x + dx, core), place(y, z, x, core)))
        return lax.ppermute(value, AXES, pairs)

    def give(value, *offsets):
        return fetch(value, *(tuple(-o for o in offset) for offset in offsets))

    def swap(value):
        return lax.ppermute(value, AXES, [(i, i ^ 1) for i in range(ny * nz * nx * 2)])

    width = embeddings.shape[1]
    ids = cluster_id.reshape(1, ROWS)
    half = call(own_kernel, "own", HALF, width, embeddings, ids)
    block = call(chip_kernel, "chip", BLOCK, width, half, swap(embeddings), swap(cluster_id).reshape(1, ROWS))

    after = lax.optimization_barrier

    key1 = fetch(block, (0, 0, 1), (0, 1, 0))
    key2 = fetch(block, (0, 0, 2), (0, 2, 0))
    near = fetch(block, (1, 0, 0), (-1, 0, 0))
    key4 = fetch(key2, (0, -1, 0), (0, 0, -1))
    far = fetch(near, (1, 0, 0), (-1, 0, 0))

    own = [(block, (OWN, OTHER))]
    sides = [whole(near), (swap(near), (OTHER, OWN))]
    beyond = [whole(far)]
    keys = [(block, (OWN,)), whole(key2)]
    (state_o,), _ = score([own], keys, own_key=True)
    key1, state_o = after((key1, state_o))
    key3 = fetch(key1, (0, -1, 0), (0, 0, 1))
    (state_s,), _ = score([sides], keys)
    (state_o, state_s), top1 = score([own, sides], [whole(key1)], [state_o, state_s], collect=0)
    key4, state_s = after((key4, state_s))
    key5 = fetch(key4[:HALF], (0, -1, 0), (0, 0, -1))
    (state_o, state_s), top4 = score([own, sides], [whole(key4)], [state_o, state_s], collect=0)
    (state_b,), tops = score([beyond], keys + [whole(key1), whole(key4)], collect=2)
    home1 = give(jnp.maximum(top1, tops[: 2 * ROWS]), (0, 0, 1), (0, 1, 0))
    home4 = give(jnp.maximum(top4, tops[2 * ROWS :]), (0, -1, 2), (0, 2, -1))
    (state_o, state_s, state_b), top3 = score([own, sides, beyond], [whole(key3)], [state_o, state_s, state_b], collect=0)
    home3 = give(top3, (0, -1, 1), (0, 1, 1))
    ((best_b, _),), _ = score([beyond], [whole(key5)], [state_b], last=True)
    ((best_s, _),), _ = score([sides], [whole(key5)], [state_s], last=True)
    ((best_o, _),), _ = score([own], [whole(key5)], [state_o], last=True)
    best_s = best_s[0].reshape(2, 2 * ROWS)

    from_far = give(best_b[0], (2, 0, 0), (2, 0, 0))
    from_up = give(best_s[0], (1, 0, 0), (-1, 0, 0))
    from_down = give(best_s[1], (-1, 0, 0), (1, 0, 0))
    home = functools.reduce(jnp.maximum, [best_o[0], home1, home4, home3, from_far, from_up, from_down])
    return jnp.maximum(home[:ROWS], swap(home[ROWS:]))


def solution(mesh):
    in_specs = (P(AXES, None), P(AXES))
    return jax.shard_map(
        per_device, mesh=mesh, in_specs=in_specs, out_specs=P(AXES), check_vma=False
    )
```

```python
import functools

import jax
import jax.numpy as jnp
from jax import lax
from jax.experimental import pallas as pl
from jax.experimental.pallas import tpu as pltpu
from jax.sharding import PartitionSpec as P

AXES = ("grp", "dev")
ROWS = 256
TAIL = 16
HALF = ROWS + TAIL
BLOCK = HALF + ROWS
SECOND = HALF
LANES = 128
FLOOR = -1.0


def unit(rows):
    values = rows.astype(jnp.float32)
    norm = jnp.sqrt(jnp.sum(values * values, axis=1, keepdims=True) + 1e-06)
    return (values / norm).astype(jnp.bfloat16)


def spread(ids):
    return jnp.broadcast_to(ids.astype(jnp.float32), (TAIL, ROWS)).astype(jnp.bfloat16)


def own_kernel(rows_ref, ids_ref, half_ref):
    half_ref[0:ROWS, :] = unit(rows_ref[...])
    half_ref[ROWS:HALF, 0:ROWS] = spread(ids_ref[...])
    half_ref[ROWS:HALF, ROWS:] = jnp.zeros((TAIL, half_ref.shape[1] - ROWS), jnp.bfloat16)


def chip_kernel(half_ref, rows_ref, ids_ref, block_ref):
    block_ref[0:HALF, :] = half_ref[...]
    block_ref[ROWS:HALF, ROWS : 2 * ROWS] = spread(ids_ref[...])
    block_ref[SECOND:BLOCK, :] = unit(rows_ref[...])


def call(kernel, name, rows, width, *operands):
    return pl.pallas_call(
        kernel,
        out_shape=jax.ShapeDtypeStruct((rows, width), jnp.bfloat16),
        compiler_params=pltpu.CompilerParams(vmem_limit_bytes=16 * 1024 * 1024),
        name=name,
    )(*operands)


OWN, OTHER = (0, 0), (SECOND, ROWS)


def whole(block):
    return (block, (OWN,) if block.shape[0] == HALF else (OWN, OTHER))


def ids_row(ref, lane):
    return ref[ROWS:HALF, lane : lane + ROWS].astype(jnp.float32)[0:1, :]


def score_kernel(groups, key_parts, n_blocks, first, last, collect, *refs):
    blocks, refs = refs[:n_blocks], list(refs[n_blocks:])
    key_parts = [(blocks[at], row, lane) for at, (row, lane) in key_parts]
    row_index = lax.broadcasted_iota(jnp.int32, (ROWS, ROWS), 0)
    col_index = lax.broadcasted_iota(jnp.int32, (ROWS, ROWS), 1)
    states = [(None, None) if first else (refs.pop(0), refs.pop(0)) for _ in groups]
    results = [(refs.pop(0), refs.pop(0) if first else column_ref) for _, column_ref in states]
    tops = {}
    for group, (query_parts, own_key) in enumerate(groups):
        before_ref, (best_ref, column_ref) = states[group][0], results[group]
        for place, (at, (row, lane)) in enumerate(query_parts):
            here = slice(place * ROWS, (place + 1) * ROWS)
            rows = blocks[at][row : row + ROWS, :]
            if first:
                ids = jnp.broadcast_to(ids_row(blocks[at], lane), (ROWS, ROWS))
                column = jnp.sum(jnp.where(row_index == col_index, ids, 0.0), axis=1, keepdims=True)
                column = jnp.broadcast_to(column, (ROWS, LANES))
                column_ref[here, :] = column
                best = jnp.full((ROWS, LANES), FLOOR, jnp.float32)
            else:
                column, best = column_ref[here, :], before_ref[here, :]
            for number, (key_ref, key_row, key_lane) in enumerate(key_parts):
                scores = lax.dot_general(
                    rows,
                    key_ref[key_row : key_row + ROWS, :],
                    (((1,), (1,)), ((), ())),
                    preferred_element_type=jnp.float32,
                )
                ids = ids_row(key_ref, key_lane)
                for start in range(0, ROWS, LANES):
                    lanes = slice(start, start + LANES)
                    match = column == ids[:, lanes]
                    if own_key and place == 0 and number == 0:
                        match = match & (row_index[:, lanes] != col_index[:, lanes])
                    kept = jnp.where(match, scores[:, lanes], FLOOR)
                    best = jnp.maximum(best, kept)
                    if number >= collect:
                        top = jnp.max(kept.reshape(ROWS // 8, 8, LANES), axis=0)
                        at_top = (number, start)
                        tops[at_top] = jnp.maximum(tops[at_top], top) if at_top in tops else top
            if last:
                best_ref[0:1, here] = jnp.max(best.T, axis=0, keepdims=True)
            else:
                best_ref[here, :] = best
    for (number, start), top in tops.items():
        at = (number - collect) * ROWS + start
        refs[0][0:1, at : at + LANES] = jnp.max(top, axis=0, keepdims=True)


def score(groups, keys, states=None, last=False, collect=None, own_key=False):
    blocks = []

    def listed(pieces):
        found = []
        for block, parts in pieces:
            at = next((i for i, b in enumerate(blocks) if b is block), len(blocks))
            if at == len(blocks):
                blocks.append(block)
            found += [(at, part) for part in parts]
        return found

    listed_groups = [(listed(group), own_key and i == 0) for i, group in enumerate(groups)]
    key_parts = listed(keys)
    counts = [len(parts) * ROWS for parts, _ in listed_groups]
    count, key_rows, width = sum(counts), len(key_parts) * ROWS, blocks[0].shape[1]
    skipped = len(key_parts) if collect is None else sum(len(parts) for _, parts in keys[:collect])
    first = states is None
    shapes = []
    for rows in counts:
        wide = jax.ShapeDtypeStruct((rows, LANES), jnp.float32)
        shapes.append(jax.ShapeDtypeStruct((1, rows), jnp.float32) if last else wide)
        if first:
            shapes.append(wide)
    if collect is not None:
        shapes.append(jax.ShapeDtypeStruct((1, key_rows - skipped * ROWS), jnp.float32))
    result = pl.pallas_call(
        functools.partial(score_kernel, listed_groups, key_parts, len(blocks), first, last, skipped),
        out_shape=tuple(shapes),
        compiler_params=pltpu.CompilerParams(vmem_limit_bytes=32 * 1024 * 1024),
        cost_estimate=pl.CostEstimate(
            flops=2 * count * key_rows * width,
            bytes_accessed=2 * width * (count + key_rows),
            transcendentals=0,
        ),
        name="score",
    )(*blocks, *(() if first else (x for state in states for x in state)))
    if first:
        states = [(result[2 * i], result[2 * i + 1]) for i in range(len(groups))]
    else:
        states = [(result[i], states[i][1]) for i in range(len(groups))]
    return states, (None if collect is None else result[-1][0])


def per_device(embeddings, cluster_id):
    ny, nz, nx = 4, 4, 4

    def place(y, z, x, core):
        return (((y % ny) * nz + z % nz) * nx + x % nx) * 2 + core

    def fetch(value, *offsets):
        pairs = []
        for y in range(ny):
            for z in range(nz):
                for x in range(nx):
                    for core, (dy, dz, dx) in enumerate(offsets):
                        pairs.append((place(y + dy, z + dz, x + dx, core), place(y, z, x, core)))
        return lax.ppermute(value, AXES, pairs)

    def give(value, *offsets):
        return fetch(value, *(tuple(-o for o in offset) for offset in offsets))

    def swap(value):
        return lax.ppermute(value, AXES, [(i, i ^ 1) for i in range(ny * nz * nx * 2)])

    width = embeddings.shape[1]
    ids = cluster_id.reshape(1, ROWS)
    half = call(own_kernel, "own", HALF, width, embeddings, ids)
    block = call(chip_kernel, "chip", BLOCK, width, half, swap(embeddings), swap(cluster_id).reshape(1, ROWS))

    after = lax.optimization_barrier

    key1 = fetch(block, (0, 0, 1), (0, 1, 0))
    key2 = fetch(block, (0, 0, 2), (0, 2, 0))
    near = fetch(block, (1, 0, 0), (-1, 0, 0))
    key4 = fetch(key2, (0, -1, 0), (0, 0, -1))
    far = fetch(near, (1, 0, 0), (-1, 0, 0))

    own = [(block, (OWN, OTHER))]
    sides = [whole(near), whole(swap(near))]
    beyond = [whole(far)]
    keys = [(block, (OWN,)), whole(key2)]
    (state_o,), _ = score([own], keys, own_key=True)
    key1, state_o = after((key1, state_o))
    key3 = fetch(key1, (0, -1, 0), (0, 0, 1))
    (state_s,), _ = score([sides], keys)
    (state_o, state_s), top1 = score([own, sides], [whole(key1)], [state_o, state_s], collect=0)
    key4, state_s = after((key4, state_s))
    key5 = fetch(key4[:HALF], (0, -1, 0), (0, 0, -1))
    (state_o, state_s), top4 = score([own, sides], [whole(key4)], [state_o, state_s], collect=0)
    (state_b,), tops = score([beyond], keys + [whole(key1), whole(key4)], collect=2)
    home1 = give(jnp.maximum(top1, tops[: 2 * ROWS]), (0, 0, 1), (0, 1, 0))
    home4 = give(jnp.maximum(top4, tops[2 * ROWS :]), (0, -1, 2), (0, 2, -1))
    (state_o, state_s, state_b), top3 = score([own, sides, beyond], [whole(key3)], [state_o, state_s, state_b], collect=0)
    home3 = give(top3, (0, -1, 1), (0, 1, 1))
    ((best_b, _),), _ = score([beyond], [whole(key5)], [state_b], last=True)
    ((best_s, _),), _ = score([sides], [whole(key5)], [state_s], last=True)
    ((best_o, _),), _ = score([own], [whole(key5)], [state_o], last=True)
    best_s = best_s[0].reshape(2, 2 * ROWS)

    from_far = give(best_b[0], (2, 0, 0), (2, 0, 0))
    sides = jnp.maximum(best_s[0], swap(best_s[1]))
    from_near = give(sides, (1, 0, 0), (-1, 0, 0))
    home = functools.reduce(jnp.maximum, [best_o[0], home1, home4, home3, from_far, from_near])
    return jnp.maximum(home[:ROWS], swap(home[ROWS:]))


def solution(mesh):
    in_specs = (P(AXES, None), P(AXES))
    return jax.shard_map(
        per_device, mesh=mesh, in_specs=in_specs, out_specs=P(AXES), check_vma=False
    )
```

```python
import functools

import jax
import jax.numpy as jnp
from jax import lax
from jax.experimental import pallas as pl
from jax.experimental.pallas import tpu as pltpu
from jax.sharding import PartitionSpec as P

AXES = ("grp", "dev")
ROWS = 256
TAIL = 16
HALF = ROWS + TAIL
BLOCK = HALF + ROWS
SECOND = HALF
LANES = 128
FLOOR = -1.0


def unit(rows):
    values = rows.astype(jnp.float32)
    norm = jnp.sqrt(jnp.sum(values * values, axis=1, keepdims=True) + 1e-06)
    return (values / norm).astype(jnp.bfloat16)


def spread(ids):
    return jnp.broadcast_to(ids.astype(jnp.float32), (TAIL, ROWS)).astype(jnp.bfloat16)


def own_kernel(rows_ref, ids_ref, half_ref):
    half_ref[0:ROWS, :] = unit(rows_ref[...])
    half_ref[ROWS:HALF, 0:ROWS] = spread(ids_ref[...])
    half_ref[ROWS:HALF, ROWS:] = jnp.zeros((TAIL, half_ref.shape[1] - ROWS), jnp.bfloat16)


def chip_kernel(half_ref, rows_ref, ids_ref, block_ref):
    block_ref[0:HALF, :] = half_ref[...]
    block_ref[ROWS:HALF, ROWS : 2 * ROWS] = spread(ids_ref[...])
    block_ref[SECOND:BLOCK, :] = unit(rows_ref[...])


def call(kernel, name, rows, width, *operands):
    return pl.pallas_call(
        kernel,
        out_shape=jax.ShapeDtypeStruct((rows, width), jnp.bfloat16),
        compiler_params=pltpu.CompilerParams(vmem_limit_bytes=16 * 1024 * 1024),
        name=name,
    )(*operands)


OWN, OTHER = (0, 0), (SECOND, ROWS)


def whole(block):
    return (block, (OWN,) if block.shape[0] == HALF else (OWN, OTHER))


def ids_row(ref, lane):
    return ref[ROWS:HALF, lane : lane + ROWS].astype(jnp.float32)[0:1, :]


def score_kernel(groups, key_parts, n_blocks, first, last, collect, *refs):
    blocks, refs = refs[:n_blocks], list(refs[n_blocks:])
    key_parts = [(blocks[at], row, lane) for at, (row, lane) in key_parts]
    row_index = lax.broadcasted_iota(jnp.int32, (ROWS, ROWS), 0)
    col_index = lax.broadcasted_iota(jnp.int32, (ROWS, ROWS), 1)
    states = [(None, None) if first else (refs.pop(0), refs.pop(0)) for _ in groups]
    results = [(refs.pop(0), refs.pop(0) if first else column_ref) for _, column_ref in states]
    tops = {}
    for group, (query_parts, own_key) in enumerate(groups):
        before_ref, (best_ref, column_ref) = states[group][0], results[group]
        for place, (at, (row, lane)) in enumerate(query_parts):
            here = slice(place * ROWS, (place + 1) * ROWS)
            rows = blocks[at][row : row + ROWS, :]
            if first:
                ids = jnp.broadcast_to(ids_row(blocks[at], lane), (ROWS, ROWS))
                column = jnp.sum(jnp.where(row_index == col_index, ids, 0.0), axis=1, keepdims=True)
                column = jnp.broadcast_to(column, (ROWS, LANES))
                column_ref[here, :] = column
                best = jnp.full((ROWS, LANES), FLOOR, jnp.float32)
            else:
                column, best = column_ref[here, :], before_ref[here, :]
            for number, (key_ref, key_row, key_lane) in enumerate(key_parts):
                scores = lax.dot_general(
                    rows,
                    key_ref[key_row : key_row + ROWS, :],
                    (((1,), (1,)), ((), ())),
                    preferred_element_type=jnp.float32,
                )
                ids = ids_row(key_ref, key_lane)
                for start in range(0, ROWS, LANES):
                    lanes = slice(start, start + LANES)
                    match = column == ids[:, lanes]
                    if own_key and place == 0 and number == 0:
                        match = match & (row_index[:, lanes] != col_index[:, lanes])
                    kept = jnp.where(match, scores[:, lanes], FLOOR)
                    best = jnp.maximum(best, kept)
                    if number >= collect:
                        top = jnp.max(kept.reshape(ROWS // 8, 8, LANES), axis=0)
                        at_top = (number, start)
                        tops[at_top] = jnp.maximum(tops[at_top], top) if at_top in tops else top
            if last:
                best_ref[0:1, here] = jnp.max(best.T, axis=0, keepdims=True)
            else:
                best_ref[here, :] = best
    for (number, start), top in tops.items():
        at = (number - collect) * ROWS + start
        refs[0][0:1, at : at + LANES] = jnp.max(top, axis=0, keepdims=True)


def score(groups, keys, states=None, last=False, collect=None, own_key=False, weight=1):
    blocks = []

    def listed(pieces):
        found = []
        for block, parts in pieces:
            at = next((i for i, b in enumerate(blocks) if b is block), len(blocks))
            if at == len(blocks):
                blocks.append(block)
            found += [(at, part) for part in parts]
        return found

    listed_groups = [(listed(group), own_key and i == 0) for i, group in enumerate(groups)]
    key_parts = listed(keys)
    counts = [len(parts) * ROWS for parts, _ in listed_groups]
    count, key_rows, width = sum(counts), len(key_parts) * ROWS, blocks[0].shape[1]
    skipped = len(key_parts) if collect is None else sum(len(parts) for _, parts in keys[:collect])
    first = states is None
    shapes = []
    for rows in counts:
        wide = jax.ShapeDtypeStruct((rows, LANES), jnp.float32)
        shapes.append(jax.ShapeDtypeStruct((1, rows), jnp.float32) if last else wide)
        if first:
            shapes.append(wide)
    if collect is not None:
        shapes.append(jax.ShapeDtypeStruct((1, key_rows - skipped * ROWS), jnp.float32))
    result = pl.pallas_call(
        functools.partial(score_kernel, listed_groups, key_parts, len(blocks), first, last, skipped),
        out_shape=tuple(shapes),
        compiler_params=pltpu.CompilerParams(vmem_limit_bytes=32 * 1024 * 1024),
        cost_estimate=pl.CostEstimate(
            flops=2 * weight * count * key_rows * width,
            bytes_accessed=2 * width * (count + key_rows),
            transcendentals=0,
        ),
        name="score",
    )(*blocks, *(() if first else (x for state in states for x in state)))
    if first:
        states = [(result[2 * i], result[2 * i + 1]) for i in range(len(groups))]
    else:
        states = [(result[i], states[i][1]) for i in range(len(groups))]
    return states, (None if collect is None else result[-1][0])


def per_device(embeddings, cluster_id):
    ny, nz, nx = 4, 4, 4

    def place(y, z, x, core):
        return (((y % ny) * nz + z % nz) * nx + x % nx) * 2 + core

    def fetch(value, *offsets):
        pairs = []
        for y in range(ny):
            for z in range(nz):
                for x in range(nx):
                    for core, (dy, dz, dx) in enumerate(offsets):
                        pairs.append((place(y + dy, z + dz, x + dx, core), place(y, z, x, core)))
        return lax.ppermute(value, AXES, pairs)

    def give(value, *offsets):
        return fetch(value, *(tuple(-o for o in offset) for offset in offsets))

    def swap(value):
        return lax.ppermute(value, AXES, [(i, i ^ 1) for i in range(ny * nz * nx * 2)])

    width = embeddings.shape[1]
    ids = cluster_id.reshape(1, ROWS)
    half = call(own_kernel, "own", HALF, width, embeddings, ids)
    block = call(chip_kernel, "chip", BLOCK, width, half, swap(embeddings), swap(cluster_id).reshape(1, ROWS))

    after = lax.optimization_barrier

    key1 = fetch(block, (0, 0, 1), (0, 1, 0))
    key2 = fetch(block, (0, 0, 2), (0, 2, 0))
    near = fetch(block, (1, 0, 0), (-1, 0, 0))
    key4 = fetch(key2, (0, -1, 0), (0, 0, -1))
    far = fetch(near, (1, 0, 0), (-1, 0, 0))

    own = [(block, (OWN, OTHER))]
    sides = [whole(near), (swap(near), (OTHER, OWN))]
    beyond = [whole(far)]
    keys = [(block, (OWN,)), whole(key2)]
    (state_o,), _ = score([own], keys, own_key=True)
    key1, state_o = after((key1, state_o))
    key3 = fetch(key1, (0, -1, 0), (0, 0, 1))
    (state_s,), _ = score([sides], keys, weight=4)
    (state_o, state_s), top1 = score([own, sides], [whole(key1)], [state_o, state_s], collect=0)
    key4, state_s = after((key4, state_s))
    key5 = fetch(key4[:HALF], (0, -1, 0), (0, 0, -1))
    (state_o, state_s), top4 = score([own, sides], [whole(key4)], [state_o, state_s], collect=0)
    (state_b,), tops = score([beyond], keys + [whole(key1), whole(key4)], collect=2)
    home1 = give(jnp.maximum(top1, tops[: 2 * ROWS]), (0, 0, 1), (0, 1, 0))
    home4 = give(jnp.maximum(top4, tops[2 * ROWS :]), (0, -1, 2), (0, 2, -1))
    (state_o, state_s, state_b), top3 = score([own, sides, beyond], [whole(key3)], [state_o, state_s, state_b], collect=0)
    home3 = give(top3, (0, -1, 1), (0, 1, 1))
    ((best_b, _),), _ = score([beyond], [whole(key5)], [state_b], last=True)
    ((best_s, _),), _ = score([sides], [whole(key5)], [state_s], last=True)
    ((best_o, _),), _ = score([own], [whole(key5)], [state_o], last=True)
    best_s = best_s[0].reshape(2, 2 * ROWS)

    from_far = give(best_b[0], (2, 0, 0), (2, 0, 0))
    from_up = give(best_s[0], (1, 0, 0), (-1, 0, 0))
    from_down = give(best_s[1], (-1, 0, 0), (1, 0, 0))
    home = functools.reduce(jnp.maximum, [best_o[0], home1, home4, home3, from_far, from_up, from_down])
    return jnp.maximum(home[:ROWS], swap(home[ROWS:]))


def solution(mesh):
    in_specs = (P(AXES, None), P(AXES))
    return jax.shard_map(
        per_device, mesh=mesh, in_specs=in_specs, out_specs=P(AXES), check_vma=False
    )
```

```python
import functools

import jax
import jax.numpy as jnp
from jax import lax
from jax.experimental import pallas as pl
from jax.experimental.pallas import tpu as pltpu
from jax.sharding import PartitionSpec as P

AXES = ("grp", "dev")
ROWS = 256
TAIL = 16
HALF = ROWS + TAIL
BLOCK = HALF + ROWS
SECOND = HALF
LANES = 128
FLOOR = -1.0


def unit(rows):
    values = rows.astype(jnp.float32)
    norm = jnp.sqrt(jnp.sum(values * values, axis=1, keepdims=True) + 1e-06)
    return (values / norm).astype(jnp.bfloat16)


def spread(ids):
    return jnp.broadcast_to(ids.astype(jnp.float32), (TAIL, ROWS)).astype(jnp.bfloat16)


def own_kernel(rows_ref, ids_ref, half_ref):
    half_ref[0:ROWS, :] = unit(rows_ref[...])
    half_ref[ROWS:HALF, 0:ROWS] = spread(ids_ref[...])
    half_ref[ROWS:HALF, ROWS:] = jnp.zeros((TAIL, half_ref.shape[1] - ROWS), jnp.bfloat16)


def chip_kernel(half_ref, rows_ref, ids_ref, block_ref):
    block_ref[0:HALF, :] = half_ref[...]
    block_ref[ROWS:HALF, ROWS : 2 * ROWS] = spread(ids_ref[...])
    block_ref[SECOND:BLOCK, :] = unit(rows_ref[...])


def call(kernel, name, rows, width, *operands):
    return pl.pallas_call(
        kernel,
        out_shape=jax.ShapeDtypeStruct((rows, width), jnp.bfloat16),
        compiler_params=pltpu.CompilerParams(vmem_limit_bytes=16 * 1024 * 1024),
        name=name,
    )(*operands)


OWN, OTHER = (0, 0), (SECOND, ROWS)


def whole(block):
    return (block, (OWN,) if block.shape[0] == HALF else (OWN, OTHER))


def ids_row(ref, lane):
    return ref[ROWS:HALF, lane : lane + ROWS].astype(jnp.float32)[0:1, :]


def score_kernel(groups, key_parts, n_blocks, first, last, collect, *refs):
    blocks, refs = refs[:n_blocks], list(refs[n_blocks:])
    key_parts = [(blocks[at], row, lane) for at, (row, lane) in key_parts]
    row_index = lax.broadcasted_iota(jnp.int32, (ROWS, ROWS), 0)
    col_index = lax.broadcasted_iota(jnp.int32, (ROWS, ROWS), 1)
    states = [(None, None) if first else (refs.pop(0), refs.pop(0)) for _ in groups]
    results = [(refs.pop(0), refs.pop(0) if first else column_ref) for _, column_ref in states]
    tops = {}
    for group, (query_parts, own_key) in enumerate(groups):
        before_ref, (best_ref, column_ref) = states[group][0], results[group]
        for place, (at, (row, lane)) in enumerate(query_parts):
            here = slice(place * ROWS, (place + 1) * ROWS)
            rows = blocks[at][row : row + ROWS, :]
            if first:
                ids = jnp.broadcast_to(ids_row(blocks[at], lane), (ROWS, ROWS))
                column = jnp.sum(jnp.where(row_index == col_index, ids, 0.0), axis=1, keepdims=True)
                column = jnp.broadcast_to(column, (ROWS, LANES))
                column_ref[here, :] = column
                best = jnp.full((ROWS, LANES), FLOOR, jnp.float32)
            else:
                column, best = column_ref[here, :], before_ref[here, :]
            for number, (key_ref, key_row, key_lane) in enumerate(key_parts):
                scores = lax.dot_general(
                    rows,
                    key_ref[key_row : key_row + ROWS, :],
                    (((1,), (1,)), ((), ())),
                    preferred_element_type=jnp.float32,
                )
                ids = ids_row(key_ref, key_lane)
                for start in range(0, ROWS, LANES):
                    lanes = slice(start, start + LANES)
                    match = column == ids[:, lanes]
                    if own_key and place == 0 and number == 0:
                        match = match & (row_index[:, lanes] != col_index[:, lanes])
                    kept = jnp.where(match, scores[:, lanes], FLOOR)
                    best = jnp.maximum(best, kept)
                    if number >= collect:
                        top = jnp.max(kept.reshape(ROWS // 8, 8, LANES), axis=0)
                        at_top = (number, start)
                        tops[at_top] = jnp.maximum(tops[at_top], top) if at_top in tops else top
            if last:
                best_ref[0:1, here] = jnp.max(best.T, axis=0, keepdims=True)
            else:
                best_ref[here, :] = best
    for (number, start), top in tops.items():
        at = (number - collect) * ROWS + start
        refs[0][0:1, at : at + LANES] = jnp.max(top, axis=0, keepdims=True)


def score(groups, keys, states=None, last=False, collect=None, own_key=False):
    blocks = []

    def listed(pieces):
        found = []
        for block, parts in pieces:
            at = next((i for i, b in enumerate(blocks) if b is block), len(blocks))
            if at == len(blocks):
                blocks.append(block)
            found += [(at, part) for part in parts]
        return found

    listed_groups = [(listed(group), own_key and i == 0) for i, group in enumerate(groups)]
    key_parts = listed(keys)
    counts = [len(parts) * ROWS for parts, _ in listed_groups]
    count, key_rows, width = sum(counts), len(key_parts) * ROWS, blocks[0].shape[1]
    skipped = len(key_parts) if collect is None else sum(len(parts) for _, parts in keys[:collect])
    first = states is None
    shapes = []
    for rows in counts:
        wide = jax.ShapeDtypeStruct((rows, LANES), jnp.float32)
        shapes.append(jax.ShapeDtypeStruct((1, rows), jnp.float32) if last else wide)
        if first:
            shapes.append(wide)
    if collect is not None:
        shapes.append(jax.ShapeDtypeStruct((1, key_rows - skipped * ROWS), jnp.float32))
    result = pl.pallas_call(
        functools.partial(score_kernel, listed_groups, key_parts, len(blocks), first, last, skipped),
        out_shape=tuple(shapes),
        compiler_params=pltpu.CompilerParams(vmem_limit_bytes=32 * 1024 * 1024),
        cost_estimate=pl.CostEstimate(
            flops=2 * count * key_rows * width,
            bytes_accessed=2 * width * (count + key_rows),
            transcendentals=0,
        ),
        name="score",
    )(*blocks, *(() if first else (x for state in states for x in state)))
    if first:
        states = [(result[2 * i], result[2 * i + 1]) for i in range(len(groups))]
    else:
        states = [(result[i], states[i][1]) for i in range(len(groups))]
    return states, (None if collect is None else result[-1][0])


def per_device(embeddings, cluster_id):
    ny, nz, nx = 4, 4, 4

    def place(y, z, x, core):
        return (((y % ny) * nz + z % nz) * nx + x % nx) * 2 + core

    def fetch(value, *offsets):
        pairs = []
        for y in range(ny):
            for z in range(nz):
                for x in range(nx):
                    for core, (dy, dz, dx) in enumerate(offsets):
                        pairs.append((place(y + dy, z + dz, x + dx, core), place(y, z, x, core)))
        return lax.ppermute(value, AXES, pairs)

    def give(value, *offsets):
        return fetch(value, *(tuple(-o for o in offset) for offset in offsets))

    def swap(value):
        return lax.ppermute(value, AXES, [(i, i ^ 1) for i in range(ny * nz * nx * 2)])

    width = embeddings.shape[1]
    ids = cluster_id.reshape(1, ROWS)
    half = call(own_kernel, "own", HALF, width, embeddings, ids)
    block = call(chip_kernel, "chip", BLOCK, width, half, swap(embeddings), swap(cluster_id).reshape(1, ROWS))

    after = lax.optimization_barrier

    key1 = fetch(block, (0, 0, 1), (0, 1, 0))
    key2 = fetch(block, (0, 0, 2), (0, 2, 0))
    near = fetch(block, (1, 0, 0), (-1, 0, 0))
    key4 = fetch(key2, (0, -1, 0), (0, 0, -1))
    far = fetch(near[:HALF], (1, 0, 0), (-1, 0, 0))

    own = [(block, (OWN, OTHER))]
    sides = [whole(near), (swap(near), (OTHER, OWN))]
    beyond = [whole(far), whole(swap(far))]
    keys = [(block, (OWN,)), whole(key2)]
    (state_o,), _ = score([own], keys, own_key=True)
    key1, state_o = after((key1, state_o))
    key3 = fetch(key1, (0, -1, 0), (0, 0, 1))
    (state_s,), _ = score([sides], keys)
    (state_o, state_s), top1 = score([own, sides], [whole(key1)], [state_o, state_s], collect=0)
    key4, state_s = after((key4, state_s))
    key5 = fetch(key4[:HALF], (0, -1, 0), (0, 0, -1))
    (state_o, state_s), top4 = score([own, sides], [whole(key4)], [state_o, state_s], collect=0)
    (state_b,), tops = score([beyond], keys + [whole(key1), whole(key4)], collect=2)
    home1 = give(jnp.maximum(top1, tops[: 2 * ROWS]), (0, 0, 1), (0, 1, 0))
    home4 = give(jnp.maximum(top4, tops[2 * ROWS :]), (0, -1, 2), (0, 2, -1))
    (state_o, state_s, state_b), top3 = score([own, sides, beyond], [whole(key3)], [state_o, state_s, state_b], collect=0)
    home3 = give(top3, (0, -1, 1), (0, 1, 1))
    ((best_b, _),), _ = score([beyond], [whole(key5)], [state_b], last=True)
    ((best_s, _),), _ = score([sides], [whole(key5)], [state_s], last=True)
    ((best_o, _),), _ = score([own], [whole(key5)], [state_o], last=True)
    best_s = best_s[0].reshape(2, 2 * ROWS)

    from_far = give(best_b[0], (2, 0, 0), (2, 0, 0))
    from_up = give(best_s[0], (1, 0, 0), (-1, 0, 0))
    from_down = give(best_s[1], (-1, 0, 0), (1, 0, 0))
    home = functools.reduce(jnp.maximum, [best_o[0], home1, home4, home3, from_far, from_up, from_down])
    return jnp.maximum(home[:ROWS], swap(home[ROWS:]))


def solution(mesh):
    in_specs = (P(AXES, None), P(AXES))
    return jax.shard_map(
        per_device, mesh=mesh, in_specs=in_specs, out_specs=P(AXES), check_vma=False
    )
```
